32 devices in a mesh: fsdp: 2 (over y), ckpt: 4 (over z), dp: 4 (over x, core).
Axes of the slice: x: 2, y: 2, z: 4, core: 2. Of those that a mesh axis runs over, the one named last changes fastest.
Arguments:
- activations: bfloat16 [4, 1536, 4096], P('ckpt', 'dp', 'fsdp'), may hold values from -6 to 6
- gate_weight: bfloat16 [4, 4096, 14336], P('ckpt', 'dp', 'fsdp'), may hold values from -0.09375 to 0.09375
- cotangent: bfloat16 [4, 1536, 14336], P('ckpt', 'dp', 'fsdp'), may hold values from -6 to 6
- sketch_left: bfloat16 [32, 4096], replicated, may hold values from -0.09375 to 0.09375
- sketch_right: bfloat16 [32, 14336], P(None, 'fsdp'), may hold values from -0.046875 to 0.046875
- landmarks: bfloat16 [4, 2048, 1024], P('ckpt', 'dp', 'fsdp'), may hold values from -0.01171875 to 0.01171875
Outputs:
- scores: float32 [12, 2048], P('dp', ('fsdp', 'ckpt'))
The draws below stay inside these ranges and needn't reach their ends.
All inputs are finite; a program needn't handle non-finite values.
Results may differ from the reference program's by a relative error of at most 0.0042.
Values may be sent and summed in bfloat16 or wider, within the bound.
No kernel may reach another device: no remote copies, remote signals or barrier semaphores. Data moves between devices by JAX's collectives and lax.ppermute only.
A program may use at most 192 MiB of HBM per device.

```python
import jax
import jax.numpy as jnp
from jax import lax

D = 4096
FF = 14336
KA = 32
KB = 32
K = 1024
SEQ = 128
TOKENS = 1536
EXAMPLES = 12
LANDMARKS = 2048
CKPTS = 4


def levels(rng, dims, pieces, least, largest):
    loudness = 1.0
    for dim, blocks in pieces:
        draws = jax.random.uniform(jax.random.fold_in(jax.random.fold_in(rng, 6), dim), (blocks,), jnp.float32, least / len(pieces), largest / len(pieces))
        loudness = loudness * jnp.repeat(jnp.exp(draws), dims[dim] // blocks).reshape((-1,) + (1,) * (len(dims) - 1 - dim))
    return loudness


def bell_draw(own_key, extent, scale, most, shards=(), held_as=jnp.bfloat16):
    array = scale * jax.random.normal(own_key, extent, jnp.float32)
    if shards:
        array = array * levels(own_key, extent, shards, -0.22, 0.18)
    return jnp.clip(array, -most, most).astype(held_as)


def setup_inputs(seed: int = 0) -> dict:
    keys = jax.random.split(jax.random.key(seed), 7)
    return {
        "activations": bell_draw(keys[0], (CKPTS, TOKENS, D), 1.0, 6.0, ((0, 4), (1, 4), (2, 2))),
        "gate_weight": bell_draw(keys[1], (CKPTS, D, FF), D ** -0.5, 0.09375, ((0, 4), (1, 4), (2, 2))),
        "cotangent": bell_draw(keys[2], (CKPTS, TOKENS, FF), 1.0, 6.0, ((0, 4), (1, 4), (2, 2))),
        "sketch_left": bell_draw(keys[3], (KA, D), D ** -0.5, 0.09375),
        "sketch_right": bell_draw(keys[4], (KB, FF), FF ** -0.5, 0.046875, ((1, 2),)),
        "landmarks": bell_draw(keys[5], (CKPTS, LANDMARKS, K), (64 * K * CKPTS) ** -0.5, 0.01171875, ((0, 4), (1, 4), (2, 2))),
    }


def one_checkpoint(running, inputs):
    activations, gate_weight, cotangent, landmarks, sketch_left, sketch_right = inputs
    preact = jnp.dot(activations, gate_weight, preferred_element_type=jnp.float32)
    grad_up = (cotangent * jax.nn.silu(preact)).astype(jnp.bfloat16)
    left_sketch = lax.dot_general(activations, sketch_left, (((1,), (1,)), ((), ())), preferred_element_type=jnp.float32)
    right_sketch = lax.dot_general(grad_up, sketch_right, (((1,), (1,)), ((), ())), preferred_element_type=jnp.float32)
    left_three = left_sketch.reshape(EXAMPLES, SEQ, KA)
    right_three = right_sketch.reshape(EXAMPLES, SEQ, KB)
    features = jnp.einsum("esa,esb->eab", left_three, right_three, precision=lax.Precision.HIGHEST)
    features_low = features.reshape(EXAMPLES, KA * KB).astype(jnp.bfloat16)
    panel_rows = lax.dot_general(features_low, landmarks, (((1,), (1,)), ((), ())), preferred_element_type=jnp.float32)
    return running + panel_rows, None


def reference(activations, gate_weight, cotangent, sketch_left, sketch_right, landmarks):
    start_value = jnp.zeros((EXAMPLES, LANDMARKS), jnp.float32)

    def stepper(running, inputs):
        return one_checkpoint(running, (inputs[0], inputs[1], inputs[2], inputs[3], sketch_left, sketch_right))

    scores, unused = lax.scan(stepper, start_value, (activations, gate_weight, cotangent, landmarks))
    return scores
```

```python
import jax
import jax.numpy as jnp
from jax import lax
from jax.sharding import PartitionSpec as P

KA = 32
KB = 32
SEQ = 128
F32 = jnp.float32


def dot(a, b, dims):
    return lax.dot_general(a, b, (dims, ((), ())), preferred_element_type=F32)


def make_per_device(n_fsdp, n_ckpt, n_dp):
    n_x = n_dp // 2
    core_pairs = [(i, i ^ 1) for i in range(n_dp)]

    def x_pairs(shift):
        return [(i, (i + 2 * shift) % n_dp) for i in range(n_dp)]

    def swap_core(value):
        return lax.ppermute(value, "dp", core_pairs)

    def shift_x(value, shift):
        return lax.ppermute(value, "dp", x_pairs(shift % n_x))

    square = n_x == 2 and n_fsdp == 2
    both = ("fsdp", "dp")
    off_pairs, on_pairs, y_pairs, y_on_pairs = [], [], [], []
    if square:
        for f in range(2):
            for d in range(n_dp):
                here = f * n_dp + d
                x_target = f * n_dp + (d + 2) % n_dp
                y_target = (1 - f) * n_dp + d
                y_pairs.append((here, y_target))
                if d // 2 == f:
                    on_pairs.append((here, x_target))
                    y_on_pairs.append((here, y_target))
                else:
                    off_pairs.append((here, x_target))

    def spread_square(rows, aligned):
        half = rows.shape[1] // 2
        first, second = rows[:, :half], rows[:, half:]
        direct = lax.ppermute(first, both, off_pairs)
        beside = lax.ppermute(second, both, y_pairs)
        passed = lax.ppermute(beside, both, on_pairs)
        got = jnp.where(aligned, direct, passed)
        partner = lax.ppermute(got, both, y_pairs)
        other = jnp.where(
            aligned,
            jnp.concatenate([got, partner], axis=1),
            jnp.concatenate([partner, got], axis=1),
        )
        own_first = lax.ppermute(first, both, y_on_pairs)
        own = jnp.where(aligned, rows, jnp.concatenate([own_first, beside], axis=1))
        return own, [other]

    def spread_general(rows, x_index, width):
        full = lax.all_gather(rows, "fsdp", axis=1, tiled=True)
        own = lax.dynamic_slice_in_dim(full, x_index * width, width, 1)
        others = []
        for shift in range(1, n_x):
            part = lax.dynamic_slice_in_dim(full, lax.rem(x_index + shift, n_x) * width, width, 1)
            others.append(shift_x(part, shift))
        return own, others

    def scatter_sum(value, axis_name, size):
        index = lax.axis_index(axis_name)
        total = lax.dynamic_index_in_dim(value, index, 1, keepdims=False)
        for shift in range(1, size):
            block = lax.dynamic_index_in_dim(value, lax.rem(index + shift, size), 1, keepdims=False)
            total = total + lax.ppermute(
                block, axis_name, [(i, (i + shift) % size) for i in range(size)]
            )
        return total

    def per_device(activations, gate_weight, cotangent, sketch_left, sketch_right, landmarks):
        f_index = lax.axis_index("fsdp")
        d_index = lax.axis_index("dp")
        x_index, core = d_index // 2, lax.rem(d_index, 2)
        rows = activations[0]
        weight = gate_weight[0]
        tokens, part = rows.shape
        depth, hidden = weight.shape
        quarter = hidden // 2
        width = 2 * depth
        examples = tokens // SEQ

        weight_mine = lax.dynamic_slice_in_dim(weight, core * quarter, quarter, 1)
        weight_theirs = swap_core(
            lax.dynamic_slice_in_dim(weight, (1 - core) * quarter, quarter, 1)
        )
        cot = cotangent[0]
        cot_mine = lax.dynamic_slice_in_dim(cot, core * quarter, quarter, 1)
        cot_theirs = swap_core(lax.dynamic_slice_in_dim(cot, (1 - core) * quarter, quarter, 1))
        right_rows = lax.dynamic_slice_in_dim(sketch_right, core * quarter, quarter, 1)

        marks = lax.all_gather(landmarks[0], "dp", axis=0, tiled=True)
        marks = lax.all_gather(marks, "fsdp", axis=1, tiled=True)

        left_part = dot(
            rows, lax.dynamic_slice_in_dim(sketch_left, f_index * part, part, 1), ((1,), (1,))
        )
        left_mine = lax.psum(left_part, "fsdp") if n_fsdp != 2 else left_part + lax.ppermute(
            left_part, "fsdp", [(0, 1), (1, 0)]
        )
        left_theirs = swap_core(left_mine)

        def product(block):
            low, high = block[:, :depth], block[:, depth:]
            mine = jnp.where(core == 0, low, high)
            theirs = jnp.where(core == 0, high, low)
            return dot(mine, weight_mine, ((1,), (0,))) + dot(theirs, weight_theirs, ((1,), (0,)))

        aligned = x_index == f_index
        own_blocks, received = [], []
        for e in range(examples):
            piece = lax.slice_in_dim(rows, e * SEQ, (e + 1) * SEQ, axis=0)
            if square:
                own, others = spread_square(piece, aligned)
            else:
                own, others = spread_general(piece, x_index, width)
            own_blocks.append(jnp.concatenate([own, swap_core(own)], axis=0))
            arrived = []
            for shift, other in enumerate(others, start=1):
                other_low = product(other).astype(jnp.bfloat16)
                arrived.append([shift_x(other_low, -shift)])
                sibling = product(swap_core(other)).astype(jnp.bfloat16)
                arrived[-1].append(shift_x(sibling, -shift))
            received.append(arrived)

        own_parts = lax.optimization_barrier([product(block) for block in own_blocks])

        features = [[], []]
        for e in range(examples):
            for side, (cot_side, left_side) in enumerate(
                ((cot_mine, left_mine), (cot_theirs, left_theirs))
            ):
                preact = own_parts[e][side * SEQ : (side + 1) * SEQ]
                for arrived in received[e]:
                    preact = preact + arrived[side].astype(F32)
                grad_up = (
                    cot_side[e * SEQ : (e + 1) * SEQ].astype(F32) * jax.nn.silu(preact)
                ).astype(jnp.bfloat16)
                right = dot(grad_up, right_rows, ((1,), (1,)))
                feature = lax.dot_general(
                    left_side[e * SEQ : (e + 1) * SEQ],
                    right,
                    (((0,), (0,)), ((), ())),
                    precision=lax.Precision.HIGHEST,
                )
                features[side].append(feature.reshape(1, KA * KB))
        stacked = jnp.concatenate(features[0] + features[1], axis=0)
        high = stacked.astype(jnp.bfloat16)
        low = (stacked - high.astype(F32)).astype(jnp.bfloat16)
        panels = dot(jnp.concatenate([high, low], axis=0), marks, ((1,), (1,)))
        panels = panels[: 2 * examples] + panels[2 * examples :]

        scores = panels[:examples] + swap_core(panels[examples:])
        marks_here = scores.shape[1] // (n_fsdp * n_ckpt)
        scores = scatter_sum(
            scores.reshape(examples, n_fsdp, n_ckpt * marks_here), "fsdp", n_fsdp
        )
        return scatter_sum(scores.reshape(examples, n_ckpt, marks_here), "ckpt", n_ckpt)

    return per_device


def solution(mesh):
    in_specs = (
        P("ckpt", "dp", "fsdp"),
        P("ckpt", "dp", "fsdp"),
        P("ckpt", "dp", "fsdp"),
        P(),
        P(None, "fsdp"),
        P("ckpt", "dp", "fsdp"),
    )
    out_specs = P("dp", ("fsdp", "ckpt"))
    per_device = make_per_device(mesh.shape["fsdp"], mesh.shape["ckpt"], mesh.shape["dp"])
    return jax.shard_map(
        per_device, mesh=mesh, in_specs=in_specs, out_specs=out_specs, check_vma=False
    )
```

```python
import jax
import jax.numpy as jnp
from jax import lax
from jax.sharding import PartitionSpec as P

KA = 32
KB = 32
SEQ = 128
F32 = jnp.float32
BF16 = jnp.bfloat16


def dot(a, b, dims):
    return lax.dot_general(a, b, (dims, ((), ())), preferred_element_type=F32)


def after(value, *earlier):
    return lax.optimization_barrier((value, *earlier))[0]


def make_per_device(n_fsdp, n_ckpt, n_dp):
    n_x = n_dp // 2
    core_pairs = [(i, i ^ 1) for i in range(n_dp)]

    def swap_core(value):
        return lax.ppermute(value, "dp", core_pairs)

    def shift_x(value, shift):
        shift = shift % n_x
        return lax.ppermute(value, "dp", [(i, (i + 2 * shift) % n_dp) for i in range(n_dp)])

    square = n_x == 2 and n_fsdp == 2
    both = ("fsdp", "dp")
    off_x, off_y, on_x, on_y = [], [], [], []
    if square:
        for f in range(2):
            for d in range(n_dp):
                here = f * n_dp + d
                by_x, by_y = (here, f * n_dp + (d + 2) % n_dp), (here, (1 - f) * n_dp + d)
                (on_x if d // 2 == f else off_x).append(by_x)
                (on_y if d // 2 == f else off_y).append(by_y)

    def spread(rows, x_index, aligned, width, cuts, marks):
        if square:
            first = cuts[0]
            stages = [lax.ppermute(rows[first[0] : first[1]], both, off_x + on_y)]
            started = start_landmarks(after(marks, stages[0]))
            for index, (lo, hi) in enumerate(cuts[1:], start=1):
                operand = jnp.where(aligned, stages[-1], after(rows, stages[-1])[lo:hi])
                if index == 2:
                    operand = after(operand, *started)
                stages.append(lax.ppermute(operand, both, off_x + on_y))

            def other(shift, cut, earlier):
                if cut + 2 == len(stages) and len(stages) == len(cuts):
                    stages.append(lax.ppermute(after(stages[-1], earlier), both, on_y))
                here, there = stages[cut], stages[cut + 1]
                if earlier is not None:
                    here, there = after((here, there), earlier)
                return jnp.where(aligned, here, there)

            def own(earlier, later):
                rest = lax.ppermute(after(rows, stages[-1], earlier)[first[1] :], both, on_y)
                begin, rest, _ = lax.optimization_barrier((stages[0], rest, later))
                return jnp.where(aligned, rows, jnp.concatenate([begin, rest], axis=0))

            return own, other, started
        full = lax.all_gather(rows, "fsdp", axis=1, tiled=True)

        def own(earlier, later):
            return lax.dynamic_slice_in_dim(after(full, later), x_index * width, width, 1)

        parts = []
        for shift in range(1, n_x):
            part = lax.dynamic_slice_in_dim(full, lax.rem(x_index + shift, n_x) * width, width, 1)
            parts.append(shift_x(part, shift))

        def other(shift, cut, earlier):
            lo, hi = cuts[cut]
            block = parts[shift - 1][lo:hi]
            return block if earlier is None else after(block, earlier)

        return own, other, []

    def start_landmarks(marks):
        return [lax.ppermute(marks, both, off_y), lax.ppermute(marks, both, on_x)]

    def cross_landmarks(started):
        return [lax.ppermute(started[0], both, on_x)] if square else []

    def gather_landmarks(marks, started, crossed, x_index, core, aligned):
        if not square:
            marks = lax.all_gather(marks, "dp", axis=0, tiled=True)
            marks = lax.all_gather(marks, "fsdp", axis=1, tiled=True)
            return lambda earlier: marks

        def assemble(earlier):
            blocks = after((marks, started[0], started[1], crossed[0]), earlier)
            mine = jnp.where(aligned, jnp.stack(blocks[:2]), jnp.stack(blocks[2:]))
            beside = lax.ppermute(mine, both, on_y + off_y)
            own = jnp.where(aligned, mine, beside)
            far = jnp.where(aligned, beside, mine)
            chips = jnp.where(x_index == 0, jnp.stack([own, far]), jnp.stack([far, own]))
            sibling = lax.ppermute(chips, "dp", core_pairs)
            cores = lax.optimization_barrier(
                [jnp.where(core == 0, chips, sibling), jnp.where(core == 0, sibling, chips)]
            )
            rows = []
            for x in range(2):
                for one in cores:
                    rows.append(jnp.concatenate([one[x, x], one[x, 1 - x]], axis=1))
            return jnp.concatenate(lax.optimization_barrier(rows), axis=0)

        return assemble

    def scatter_sum(value, axis_name, size):
        index = lax.axis_index(axis_name)
        total = lax.dynamic_index_in_dim(value, index, 1, keepdims=False)
        for shift in range(1, size):
            block = lax.dynamic_index_in_dim(value, lax.rem(index + shift, size), 1, keepdims=False)
            total = total + lax.ppermute(
                block, axis_name, [(i, (i + shift) % size) for i in range(size)]
            )
        return total

    def per_device(activations, gate_weight, cotangent, sketch_left, sketch_right, landmarks):
        f_index = lax.axis_index("fsdp")
        d_index = lax.axis_index("dp")
        x_index, core = d_index // 2, lax.rem(d_index, 2)
        aligned = x_index == f_index
        rows, weight, cot = activations[0], gate_weight[0], cotangent[0]
        tokens, part = rows.shape
        depth = weight.shape[0]
        examples = tokens // SEQ

        weight_sibling = swap_core(weight)
        cuts = [(e * SEQ, (e + 1) * SEQ) for e in range(examples)]
        own, other, started = spread(
            rows, x_index, aligned, 2 * depth, cuts, landmarks[0]
        )
        crossed = cross_landmarks(started)
        assemble = gather_landmarks(landmarks[0], started, crossed, x_index, core, aligned)

        def split(block):
            low, high = block[:, :depth], block[:, depth:]
            return jnp.where(core == 0, low, high), jnp.where(core == 0, high, low)

        def product(block, h0=0, h1=weight.shape[1]):
            mine, theirs = split(block)
            return dot(mine, weight[:, h0:h1], ((1,), (0,))) + dot(
                theirs, weight_sibling[:, h0:h1], ((1,), (0,))
            )

        def partials(cut, lo, hi, earlier, h0=0, h1=weight.shape[1]):
            return [
                product(other(shift, cut, earlier)[lo:hi], h0, h1).astype(BF16)
                for shift in range(1, n_x)
            ]

        def send(values, earlier=None):
            if earlier is not None:
                values = [after(value, *earlier) for value in values]
            return [shift_x(value, -shift) for shift, value in enumerate(values, start=1)]

        half, hidden = SEQ // 2, weight.shape[1]
        part_a = partials(0, 0, SEQ, None, 0, hidden // 2)
        got_a = send(part_a)
        part_b = partials(0, 0, SEQ, part_a, hidden // 2, hidden)
        got_b = send(part_b)
        part_c = partials(1, 0, SEQ, part_b + crossed)
        got_c = send(part_c, got_a + got_b)
        part_d = partials(2, 0, half, got_b)
        got_d = send(part_d, got_c)
        part_e = partials(2, half, SEQ, part_d)
        got_e = send(part_e, got_c)
        marks = assemble(got_b[0])
        left = dot(
            after(rows, got_b[0]),
            lax.dynamic_slice_in_dim(sketch_left, f_index * part, part, 1),
            ((1,), (1,)),
        )
        if n_fsdp == 2:
            left = left + lax.ppermute(left, "fsdp", [(0, 1), (1, 0)])
        else:
            left = lax.psum(left, "fsdp")

        mine, theirs = split(own(part_c[0], part_e[0]))
        own_part = dot(mine, weight, ((1,), (0,)))
        theirs = after(theirs, own_part, *got_c)
        own_part = own_part + dot(theirs, weight_sibling, ((1,), (0,)))
        own_part, marks, left = lax.optimization_barrier((own_part, marks, left))

        def right_part(got, lo, hi, h0=0, h1=hidden):
            preact = own_part[lo:hi, h0:h1]
            for piece in got:
                preact = preact + piece.astype(F32)
            grad_up = (cot[lo:hi, h0:h1].astype(F32) * jax.nn.silu(preact)).astype(BF16)
            return dot(grad_up, sketch_right[:, h0:h1], ((1,), (1,)))

        rights = [
            right_part(got_a, 0, SEQ, 0, hidden // 2) + right_part(got_b, 0, SEQ, hidden // 2),
            right_part(got_c, SEQ, 2 * SEQ),
            right_part(got_d, 2 * SEQ, 2 * SEQ + half),
            right_part(got_e, 2 * SEQ + half, 3 * SEQ),
        ]
        right = jnp.concatenate(rights, axis=0).reshape(examples, SEQ, KB)
        features = jnp.einsum(
            "esa,esb->eab",
            left.reshape(examples, SEQ, KA),
            right,
            precision=lax.Precision.HIGHEST,
        ).reshape(examples, KA * KB)
        high = lax.reduce_precision(features, 8, 7)
        pair = jnp.concatenate([high, features - high], axis=0).astype(BF16)
        panels = dot(pair, marks, ((1,), (1,)))
        scores = panels[:examples] + panels[examples:]

        here = scores.shape[1] // (n_fsdp * n_ckpt)
        scores = scatter_sum(scores.reshape(examples, n_fsdp, n_ckpt * here), "fsdp", n_fsdp)
        return scatter_sum(scores.reshape(examples, n_ckpt, here), "ckpt", n_ckpt)

    return per_device


def solution(mesh):
    in_specs = (
        P("ckpt", "dp", "fsdp"),
        P("ckpt", "dp", "fsdp"),
        P("ckpt", "dp", "fsdp"),
        P(),
        P(None, "fsdp"),
        P("ckpt", "dp", "fsdp"),
    )
    out_specs = P("dp", ("fsdp", "ckpt"))
    per_device = make_per_device(mesh.shape["fsdp"], mesh.shape["ckpt"], mesh.shape["dp"])
    return jax.shard_map(
        per_device, mesh=mesh, in_specs=in_specs, out_specs=out_specs, check_vma=False
    )
```

```python
import jax
import jax.numpy as jnp
from jax import lax
from jax.sharding import PartitionSpec as P

KA = 32
KB = 32
SEQ = 128
F32 = jnp.float32
BF16 = jnp.bfloat16


def dot(a, b, dims):
    return lax.dot_general(a, b, (dims, ((), ())), preferred_element_type=F32)


def after(value, *earlier):
    return lax.optimization_barrier((value, *earlier))[0]


def make_per_device(n_fsdp, n_ckpt, n_dp):
    n_x = n_dp // 2
    core_pairs = [(i, i ^ 1) for i in range(n_dp)]

    def swap_core(value):
        return lax.ppermute(value, "dp", core_pairs)

    def shift_x(value, shift):
        shift = shift % n_x
        return lax.ppermute(value, "dp", [(i, (i + 2 * shift) % n_dp) for i in range(n_dp)])

    square = n_x == 2 and n_fsdp == 2
    both = ("fsdp", "dp")
    off_x, off_y, on_x, on_y = [], [], [], []
    if square:
        for f in range(2):
            for d in range(n_dp):
                here = f * n_dp + d
                by_x, by_y = (here, f * n_dp + (d + 2) % n_dp), (here, (1 - f) * n_dp + d)
                (on_x if d // 2 == f else off_x).append(by_x)
                (on_y if d // 2 == f else off_y).append(by_y)

    def spread(rows, x_index, aligned, width, cuts, marks):
        if square:
            first = cuts[0]
            stages = [lax.ppermute(rows[first[0] : first[1]], both, off_x + on_y)]
            started = start_landmarks(after(marks, stages[0]))
            for lo, hi in cuts[1:]:
                operand = jnp.where(aligned, stages[-1], after(rows, stages[-1])[lo:hi])
                stages.append(lax.ppermute(operand, both, off_x + on_y))

            def other(shift, cut, earlier):
                if cut + 2 == len(stages) and len(stages) == len(cuts):
                    stages.append(lax.ppermute(after(stages[-1], earlier), both, on_y))
                here, there = stages[cut], stages[cut + 1]
                if earlier is not None:
                    here, there = after((here, there), earlier)
                return jnp.where(aligned, here, there)

            def own(earlier, later):
                rest = lax.ppermute(after(rows, stages[-1], earlier)[first[1] :], both, on_y)
                begin, rest, _ = lax.optimization_barrier((stages[0], rest, later))
                return jnp.where(aligned, rows, jnp.concatenate([begin, rest], axis=0))

            return own, other, started
        full = lax.all_gather(rows, "fsdp", axis=1, tiled=True)

        def own(earlier, later):
            return lax.dynamic_slice_in_dim(after(full, later), x_index * width, width, 1)

        parts = []
        for shift in range(1, n_x):
            part = lax.dynamic_slice_in_dim(full, lax.rem(x_index + shift, n_x) * width, width, 1)
            parts.append(shift_x(part, shift))

        def other(shift, cut, earlier):
            lo, hi = cuts[cut]
            block = parts[shift - 1][lo:hi]
            return block if earlier is None else after(block, earlier)

        return own, other, []

    def start_landmarks(marks):
        return [lax.ppermute(marks, both, off_y), lax.ppermute(marks, both, on_x)]

    def cross_landmarks(started):
        return [lax.ppermute(started[0], both, on_x)] if square else []

    def gather_landmarks(marks, started, crossed, x_index, core, aligned):
        if not square:
            marks = lax.all_gather(marks, "dp", axis=0, tiled=True)
            marks = lax.all_gather(marks, "fsdp", axis=1, tiled=True)
            return lambda earlier: [marks]

        def assemble(earlier):
            blocks = after((marks, started[0], started[1], crossed[0]), earlier)
            mine = jnp.where(aligned, jnp.stack(blocks[:2]), jnp.stack(blocks[2:]))
            beside = lax.ppermute(mine, both, on_y + off_y)
            own = jnp.where(aligned, mine, beside)
            far = jnp.where(aligned, beside, mine)
            chips = jnp.where(x_index == 0, jnp.stack([own, far]), jnp.stack([far, own]))
            sibling = lax.ppermute(chips, "dp", core_pairs)
            cores = lax.optimization_barrier(
                [jnp.where(core == 0, chips, sibling), jnp.where(core == 0, sibling, chips)]
            )
            rows = []
            for x in range(2):
                for one in cores:
                    rows.append(jnp.concatenate([one[x, x], one[x, 1 - x]], axis=1))
            return lax.optimization_barrier(rows)

        return assemble

    def scatter_sum(value, axis_name, size):
        index = lax.axis_index(axis_name)
        total = lax.dynamic_index_in_dim(value, index, 1, keepdims=False)
        for shift in range(1, size):
            block = lax.dynamic_index_in_dim(value, lax.rem(index + shift, size), 1, keepdims=False)
            total = total + lax.ppermute(
                block, axis_name, [(i, (i + shift) % size) for i in range(size)]
            )
        return total

    def per_device(activations, gate_weight, cotangent, sketch_left, sketch_right, landmarks):
        f_index = lax.axis_index("fsdp")
        d_index = lax.axis_index("dp")
        x_index, core = d_index // 2, lax.rem(d_index, 2)
        aligned = x_index == f_index
        rows, weight, cot = activations[0], gate_weight[0], cotangent[0]
        tokens, part = rows.shape
        depth = weight.shape[0]
        examples = tokens // SEQ

        weight_sibling = swap_core(weight)
        cuts = [(e * SEQ, (e + 1) * SEQ) for e in range(examples)]
        own, other, started = spread(
            rows, x_index, aligned, 2 * depth, cuts, landmarks[0]
        )
        crossed = cross_landmarks(started)
        assemble = gather_landmarks(landmarks[0], started, crossed, x_index, core, aligned)

        def split(block):
            low, high = block[:, :depth], block[:, depth:]
            return jnp.where(core == 0, low, high), jnp.where(core == 0, high, low)

        def product(block, h0=0, h1=weight.shape[1]):
            mine, theirs = split(block)
            return dot(mine, weight[:, h0:h1], ((1,), (0,))) + dot(
                theirs, weight_sibling[:, h0:h1], ((1,), (0,))
            )

        def partials(cut, lo, hi, earlier, h0=0, h1=weight.shape[1]):
            return [
                product(other(shift, cut, earlier)[lo:hi], h0, h1).astype(BF16)
                for shift in range(1, n_x)
            ]

        def send(values, earlier=None):
            if earlier is not None:
                values = [after(value, *earlier) for value in values]
            return [shift_x(value, -shift) for shift, value in enumerate(values, start=1)]

        most, hidden = 3 * SEQ // 4, weight.shape[1]
        part_a = partials(0, 0, SEQ, started[:1] or None, 0, hidden // 2)
        got_a = send(part_a)
        part_b = partials(0, 0, SEQ, part_a + started, hidden // 2, hidden)
        got_b = send(part_b)
        part_c = partials(1, 0, SEQ, part_b + crossed)
        part_de = partials(2, 0, SEQ, part_c)
        part_d = [value[:most] for value in part_de]
        part_e = [value[most:] for value in part_de]
        got_c = send(part_c, got_a + got_b + part_d + part_e)
        got_d = send(part_d, got_c)
        got_e = send(part_e, got_c)
        mark_rows = assemble(got_b[0])
        mine, theirs = split(own(part_c[0], got_b[0]))
        own_part = dot(mine, weight, ((1,), (0,)))
        left = dot(
            after(rows, own_part),
            lax.dynamic_slice_in_dim(sketch_left, f_index * part, part, 1),
            ((1,), (1,)),
        )
        if n_fsdp == 2:
            left = left + lax.ppermute(left, "fsdp", [(0, 1), (1, 0)])
        else:
            left = lax.psum(left, "fsdp")
        theirs = after(theirs, own_part, *got_c)
        own_part = own_part + dot(theirs, weight_sibling, ((1,), (0,)))
        own_part, left = lax.optimization_barrier((own_part, left))

        def right_part(got, lo, hi, h0=0, h1=hidden):
            preact = own_part[lo:hi, h0:h1]
            for piece in got:
                preact = preact + piece.astype(F32)
            grad_up = (cot[lo:hi, h0:h1].astype(F32) * jax.nn.silu(preact)).astype(BF16)
            return dot(grad_up, sketch_right[:, h0:h1], ((1,), (1,)))

        rights = [
            right_part(got_a, 0, SEQ, 0, hidden // 2) + right_part(got_b, 0, SEQ, hidden // 2)
        ]
        for got, lo, hi in (
            (got_c, SEQ, 2 * SEQ),
            (got_d, 2 * SEQ, 2 * SEQ + most),
            (got_e, 2 * SEQ + most, 3 * SEQ),
        ):
            rights.append(right_part([after(value, rights[-1], *mark_rows) for value in got], lo, hi))
        marks = jnp.concatenate(mark_rows, axis=0)
        right = jnp.concatenate(rights, axis=0).reshape(examples, SEQ, KB)
        features = jnp.einsum(
            "esa,esb->eab",
            left.reshape(examples, SEQ, KA),
            right,
            precision=lax.Precision.HIGHEST,
        ).reshape(examples, KA * KB)
        high = lax.reduce_precision(features, 8, 7)
        pair = jnp.concatenate([high, features - high], axis=0).astype(BF16)
        panels = dot(pair, marks, ((1,), (1,)))
        scores = panels[:examples] + panels[examples:]

        here = scores.shape[1] // (n_fsdp * n_ckpt)
        scores = scatter_sum(scores.reshape(examples, n_fsdp, n_ckpt * here), "fsdp", n_fsdp)
        return scatter_sum(scores.reshape(examples, n_ckpt, here), "ckpt", n_ckpt)

    return per_device


def solution(mesh):
    in_specs = (
        P("ckpt", "dp", "fsdp"),
        P("ckpt", "dp", "fsdp"),
        P("ckpt", "dp", "fsdp"),
        P(),
        P(None, "fsdp"),
        P("ckpt", "dp", "fsdp"),
    )
    out_specs = P("dp", ("fsdp", "ckpt"))
    per_device = make_per_device(mesh.shape["fsdp"], mesh.shape["ckpt"], mesh.shape["dp"])
    return jax.shard_map(
        per_device, mesh=mesh, in_specs=in_specs, out_specs=out_specs, check_vma=False
    )
```

```python
import jax
import jax.numpy as jnp
from jax import lax
from jax.sharding import PartitionSpec as P

KA = 32
KB = 32
SEQ = 128
F32 = jnp.float32
BF16 = jnp.bfloat16


def dot(a, b, dims):
    return lax.dot_general(a, b, (dims, ((), ())), preferred_element_type=F32)


def after(value, *earlier):
    return lax.optimization_barrier((value, *earlier))[0]


def make_per_device(n_fsdp, n_ckpt, n_dp):
    n_x = n_dp // 2
    core_pairs = [(i, i ^ 1) for i in range(n_dp)]

    def swap_core(value):
        return lax.ppermute(value, "dp", core_pairs)

    def shift_x(value, shift):
        shift = shift % n_x
        return lax.ppermute(value, "dp", [(i, (i + 2 * shift) % n_dp) for i in range(n_dp)])

    square = n_x == 2 and n_fsdp == 2
    both = ("fsdp", "dp")
    off_x, off_y, on_x, on_y = [], [], [], []
    if square:
        for f in range(2):
            for d in range(n_dp):
                here = f * n_dp + d
                by_x, by_y = (here, f * n_dp + (d + 2) % n_dp), (here, (1 - f) * n_dp + d)
                (on_x if d // 2 == f else off_x).append(by_x)
                (on_y if d // 2 == f else off_y).append(by_y)

    def spread(rows, x_index, aligned, width, cuts, marks):
        if square:
            first = cuts[0]
            stages = [lax.ppermute(rows[first[0] : first[1]], both, off_x + on_y)]
            started = start_landmarks(after(marks, stages[0]))
            for lo, hi in cuts[1:]:
                operand = jnp.where(aligned, stages[-1], after(rows, stages[-1])[lo:hi])
                stages.append(lax.ppermute(operand, both, off_x + on_y))

            def other(shift, cut, earlier):
                if cut + 2 == len(stages) and len(stages) == len(cuts):
                    stages.append(lax.ppermute(after(stages[-1], earlier), both, on_y))
                here, there = stages[cut], stages[cut + 1]
                if earlier is not None:
                    here, there = after((here, there), earlier)
                return jnp.where(aligned, here, there)

            def own(earlier, later):
                rest = lax.ppermute(after(rows, stages[-1], earlier)[first[1] :], both, on_y)
                begin, rest, _ = lax.optimization_barrier((stages[0], rest, later))
                return jnp.where(aligned, rows, jnp.concatenate([begin, rest], axis=0))

            return own, other, started
        full = lax.all_gather(rows, "fsdp", axis=1, tiled=True)

        def own(earlier, later):
            return lax.dynamic_slice_in_dim(after(full, later), x_index * width, width, 1)

        parts = []
        for shift in range(1, n_x):
            part = lax.dynamic_slice_in_dim(full, lax.rem(x_index + shift, n_x) * width, width, 1)
            parts.append(shift_x(part, shift))

        def other(shift, cut, earlier):
            lo, hi = cuts[cut]
            block = parts[shift - 1][lo:hi]
            return block if earlier is None else after(block, earlier)

        return own, other, []

    def start_landmarks(marks):
        return [lax.ppermute(marks, both, off_y), lax.ppermute(marks, both, on_x)]

    def cross_landmarks(started):
        return [lax.ppermute(started[0], both, on_x)] if square else []

    def gather_landmarks(marks, started, crossed, x_index, core, aligned):
        if not square:
            marks = lax.all_gather(marks, "dp", axis=0, tiled=True)
            marks = lax.all_gather(marks, "fsdp", axis=1, tiled=True)
            return lambda earlier: [marks]

        def assemble(earlier):
            blocks = after((marks, started[0], started[1], crossed[0]), earlier)
            mine = jnp.where(aligned, jnp.stack(blocks[:2]), jnp.stack(blocks[2:]))
            beside = lax.ppermute(mine, both, on_y + off_y)
            own = jnp.where(aligned, mine, beside)
            far = jnp.where(aligned, beside, mine)
            chips = jnp.where(x_index == 0, jnp.stack([own, far]), jnp.stack([far, own]))
            sibling = lax.ppermute(chips, "dp", core_pairs)
            cores = lax.optimization_barrier(
                [jnp.where(core == 0, chips, sibling), jnp.where(core == 0, sibling, chips)]
            )
            rows = []
            for x in range(2):
                for one in cores:
                    rows.append(jnp.concatenate([one[x, x], one[x, 1 - x]], axis=1))
            return lax.optimization_barrier(rows)

        return assemble

    def scatter_sum(value, axis_name, size):
        index = lax.axis_index(axis_name)
        total = lax.dynamic_index_in_dim(value, index, 1, keepdims=False)
        for shift in range(1, size):
            block = lax.dynamic_index_in_dim(value, lax.rem(index + shift, size), 1, keepdims=False)
            total = total + lax.ppermute(
                block, axis_name, [(i, (i + shift) % size) for i in range(size)]
            )
        return total

    def per_device(activations, gate_weight, cotangent, sketch_left, sketch_right, landmarks):
        f_index = lax.axis_index("fsdp")
        d_index = lax.axis_index("dp")
        x_index, core = d_index // 2, lax.rem(d_index, 2)
        aligned = x_index == f_index
        rows, weight, cot = activations[0], gate_weight[0], cotangent[0]
        tokens, part = rows.shape
        depth = weight.shape[0]
        examples = tokens // SEQ

        weight_sibling = swap_core(weight)
        cuts = [(e * SEQ, (e + 1) * SEQ) for e in range(examples)]
        own, other, started = spread(
            rows, x_index, aligned, 2 * depth, cuts, landmarks[0]
        )
        crossed = cross_landmarks(started)
        assemble = gather_landmarks(landmarks[0], started, crossed, x_index, core, aligned)

        def split(block):
            low, high = block[:, :depth], block[:, depth:]
            return jnp.where(core == 0, low, high), jnp.where(core == 0, high, low)

        def product(block, h0=0, h1=weight.shape[1]):
            mine, theirs = split(block)
            return dot(mine, weight[:, h0:h1], ((1,), (0,))) + dot(
                theirs, weight_sibling[:, h0:h1], ((1,), (0,))
            )

        def partials(cut, lo, hi, earlier, h0=0, h1=weight.shape[1]):
            return [
                product(other(shift, cut, earlier)[lo:hi], h0, h1).astype(BF16)
                for shift in range(1, n_x)
            ]

        def send(values, earlier=None):
            if earlier is not None:
                values = [after(value, *earlier) for value in values]
            return [shift_x(value, -shift) for shift, value in enumerate(values, start=1)]

        most, hidden = 3 * SEQ // 4, weight.shape[1]
        part_a = partials(0, 0, SEQ, started[:1] or None, 0, hidden // 2)
        got_a = send(part_a)
        part_b = partials(0, 0, SEQ, part_a + started, hidden // 2, hidden)
        got_b = send(part_b)
        part_c = partials(1, 0, SEQ, part_b + crossed)
        part_de = partials(2, 0, SEQ, part_c)
        part_d = [value[:most] for value in part_de]
        part_e = [value[most:] for value in part_de]
        got_c = send(part_c, got_a + got_b + part_d + part_e)
        got_d = send(part_d, got_c)
        mark_rows = assemble(got_b[0])
        mine, theirs = split(own(part_c[0], got_b[0]))
        own_part = dot(mine, weight, ((1,), (0,)))
        left = dot(
            after(rows, own_part),
            lax.dynamic_slice_in_dim(sketch_left, f_index * part, part, 1),
            ((1,), (1,)),
        )
        if n_fsdp == 2:
            left = left + lax.ppermute(left, "fsdp", [(0, 1), (1, 0)])
        else:
            left = lax.psum(left, "fsdp")
        theirs = after(theirs, own_part, *got_c)
        own_part = own_part + dot(theirs, weight_sibling, ((1,), (0,)))
        own_part, left = lax.optimization_barrier((own_part, left))
        got_e = send(part_e, got_c + [own_part])

        def right_part(got, lo, hi, h0=0, h1=hidden):
            preact = own_part[lo:hi, h0:h1]
            for piece in got:
                preact = preact + piece.astype(F32)
            grad_up = (cot[lo:hi, h0:h1].astype(F32) * jax.nn.silu(preact)).astype(BF16)
            return dot(grad_up, sketch_right[:, h0:h1], ((1,), (1,)))

        rights = [
            right_part(got_a, 0, SEQ, 0, hidden // 2) + right_part(got_b, 0, SEQ, hidden // 2)
        ]
        for got, lo, hi in (
            (got_c, SEQ, 2 * SEQ),
            (got_d, 2 * SEQ, 2 * SEQ + most),
            (got_e, 2 * SEQ + most, 3 * SEQ),
        ):
            rights.append(right_part([after(value, rights[-1], *mark_rows) for value in got], lo, hi))
        marks = jnp.concatenate(mark_rows, axis=0)
        right = jnp.concatenate(rights, axis=0).reshape(examples, SEQ, KB)
        features = jnp.einsum(
            "esa,esb->eab",
            left.reshape(examples, SEQ, KA),
            right,
            precision=lax.Precision.HIGHEST,
        ).reshape(examples, KA * KB)
        high = lax.reduce_precision(features, 8, 7)
        pair = jnp.concatenate([high, features - high], axis=0).astype(BF16)
        panels = dot(pair, marks, ((1,), (1,)))
        scores = panels[:examples] + panels[examples:]

        here = scores.shape[1] // (n_fsdp * n_ckpt)
        scores = scatter_sum(scores.reshape(examples, n_fsdp, n_ckpt * here), "fsdp", n_fsdp)
        return scatter_sum(scores.reshape(examples, n_ckpt, here), "ckpt", n_ckpt)

    return per_device


def solution(mesh):
    in_specs = (
        P("ckpt", "dp", "fsdp"),
        P("ckpt", "dp", "fsdp"),
        P("ckpt", "dp", "fsdp"),
        P(),
        P(None, "fsdp"),
        P("ckpt", "dp", "fsdp"),
    )
    out_specs = P("dp", ("fsdp", "ckpt"))
    per_device = make_per_device(mesh.shape["fsdp"], mesh.shape["ckpt"], mesh.shape["dp"])
    return jax.shard_map(
        per_device, mesh=mesh, in_specs=in_specs, out_specs=out_specs, check_vma=False
    )
```

```python
import jax
import jax.numpy as jnp
from jax import lax
from jax.sharding import PartitionSpec as P

KA = 32
KB = 32
SEQ = 128
F32 = jnp.float32
BF16 = jnp.bfloat16


def dot(a, b, dims):
    return lax.dot_general(a, b, (dims, ((), ())), preferred_element_type=F32)


def after(value, *earlier):
    return lax.optimization_barrier((value, *earlier))[0]


def make_per_device(n_fsdp, n_ckpt, n_dp):
    n_x = n_dp // 2
    core_pairs = [(i, i ^ 1) for i in range(n_dp)]

    def swap_core(value):
        return lax.ppermute(value, "dp", core_pairs)

    def shift_x(value, shift):
        shift = shift % n_x
        return lax.ppermute(value, "dp", [(i, (i + 2 * shift) % n_dp) for i in range(n_dp)])

    square = n_x == 2 and n_fsdp == 2
    both = ("fsdp", "dp")
    off_x, off_y, on_x, on_y = [], [], [], []
    if square:
        for f in range(2):
            for d in range(n_dp):
                here = f * n_dp + d
                by_x, by_y = (here, f * n_dp + (d + 2) % n_dp), (here, (1 - f) * n_dp + d)
                (on_x if d // 2 == f else off_x).append(by_x)
                (on_y if d // 2 == f else off_y).append(by_y)

    def spread(rows, x_index, aligned, width, cuts, marks):
        if square:
            first = cuts[0]
            stages = [lax.ppermute(rows[first[0] : first[1]], both, off_x + on_y)]
            started = start_landmarks(after(marks, stages[0]))
            for lo, hi in cuts[1:]:
                operand = jnp.where(aligned, stages[-1], after(rows, stages[-1])[lo:hi])
                stages.append(lax.ppermute(operand, both, off_x + on_y))

            def other(shift, cut, earlier):
                if cut + 2 == len(stages) and len(stages) == len(cuts):
                    stages.append(lax.ppermute(after(stages[-1], earlier), both, on_y))
                here, there = stages[cut], stages[cut + 1]
                if earlier is not None:
                    here, there = after((here, there), earlier)
                return jnp.where(aligned, here, there)

            def own(earlier, later):
                rest = lax.ppermute(after(rows, stages[-1], earlier)[first[1] :], both, on_y)
                begin, rest, _ = lax.optimization_barrier((stages[0], rest, later))
                return jnp.where(aligned, rows, jnp.concatenate([begin, rest], axis=0))

            return own, other, started
        full = lax.all_gather(rows, "fsdp", axis=1, tiled=True)

        def own(earlier, later):
            return lax.dynamic_slice_in_dim(after(full, later), x_index * width, width, 1)

        parts = []
        for shift in range(1, n_x):
            part = lax.dynamic_slice_in_dim(full, lax.rem(x_index + shift, n_x) * width, width, 1)
            parts.append(shift_x(part, shift))

        def other(shift, cut, earlier):
            lo, hi = cuts[cut]
            block = parts[shift - 1][lo:hi]
            return block if earlier is None else after(block, earlier)

        return own, other, []

    def start_landmarks(marks):
        return [lax.ppermute(marks, both, off_y), lax.ppermute(marks, both, on_x)]

    def cross_landmarks(started):
        return [lax.ppermute(started[0], both, on_x)] if square else []

    def gather_landmarks(marks, started, crossed, x_index, core, aligned):
        if not square:
            marks = lax.all_gather(marks, "dp", axis=0, tiled=True)
            marks = lax.all_gather(marks, "fsdp", axis=1, tiled=True)
            return lambda earlier: [marks]

        def assemble(earlier):
            blocks = after((marks, started[0], started[1], crossed[0]), earlier)
            mine = jnp.where(aligned, jnp.stack(blocks[:2]), jnp.stack(blocks[2:]))
            beside = lax.ppermute(mine, both, on_y + off_y)
            own = jnp.where(aligned, mine, beside)
            far = jnp.where(aligned, beside, mine)
            chips = jnp.where(x_index == 0, jnp.stack([own, far]), jnp.stack([far, own]))
            sibling = lax.ppermute(chips, "dp", core_pairs)
            cores = lax.optimization_barrier(
                [jnp.where(core == 0, chips, sibling), jnp.where(core == 0, sibling, chips)]
            )
            rows = []
            for x in range(2):
                for one in cores:
                    rows.append(jnp.concatenate([one[x, x], one[x, 1 - x]], axis=1))
            return lax.optimization_barrier(rows)

        return assemble

    def scatter_sum(value, axis_name, size):
        index = lax.axis_index(axis_name)
        total = lax.dynamic_index_in_dim(value, index, 1, keepdims=False)
        for shift in range(1, size):
            block = lax.dynamic_index_in_dim(value, lax.rem(index + shift, size), 1, keepdims=False)
            total = total + lax.ppermute(
                block, axis_name, [(i, (i + shift) % size) for i in range(size)]
            )
        return total

    def per_device(activations, gate_weight, cotangent, sketch_left, sketch_right, landmarks):
        f_index = lax.axis_index("fsdp")
        d_index = lax.axis_index("dp")
        x_index, core = d_index // 2, lax.rem(d_index, 2)
        aligned = x_index == f_index
        rows, weight, cot = activations[0], gate_weight[0], cotangent[0]
        tokens, part = rows.shape
        depth = weight.shape[0]
        examples = tokens // SEQ

        weight_sibling = swap_core(weight)
        cuts = [(e * SEQ, (e + 1) * SEQ) for e in range(examples)]
        own, other, started = spread(
            rows, x_index, aligned, 2 * depth, cuts, landmarks[0]
        )
        crossed = cross_landmarks(started)
        assemble = gather_landmarks(landmarks[0], started, crossed, x_index, core, aligned)

        def split(block):
            low, high = block[:, :depth], block[:, depth:]
            return jnp.where(core == 0, low, high), jnp.where(core == 0, high, low)

        def product(block, h0=0, h1=weight.shape[1]):
            mine, theirs = split(block)
            return dot(mine, weight[:, h0:h1], ((1,), (0,))) + dot(
                theirs, weight_sibling[:, h0:h1], ((1,), (0,))
            )

        def partials(cut, lo, hi, earlier, h0=0, h1=weight.shape[1]):
            return [
                product(other(shift, cut, earlier)[lo:hi], h0, h1).astype(BF16)
                for shift in range(1, n_x)
            ]

        def send(values, earlier=None):
            if earlier is not None:
                values = [after(value, *earlier) for value in values]
            return [shift_x(value, -shift) for shift, value in enumerate(values, start=1)]

        most, hidden = 3 * SEQ // 4, weight.shape[1]
        part_a = partials(0, 0, SEQ, started[:1] or None, 0, hidden // 2)
        got_a = send(part_a)
        part_b = partials(0, 0, SEQ, part_a + started, hidden // 2, hidden)
        got_b = send(part_b)
        part_c = partials(1, 0, SEQ, part_b + crossed)
        part_de = partials(2, 0, SEQ, part_c)
        part_d = [value[:most] for value in part_de]
        part_e = [value[most:] for value in part_de]
        got_c = send(part_c, got_a + part_d + part_e)
        mark_rows = assemble(part_e[0])
        mine, theirs = split(own(part_c[0], got_b[0]))
        own_part = dot(mine, weight, ((1,), (0,)))
        got_d = send(part_d, got_b + [own_part])
        left = dot(
            after(rows, own_part),
            lax.dynamic_slice_in_dim(sketch_left, f_index * part, part, 1),
            ((1,), (1,)),
        )
        if n_fsdp == 2:
            left = left + lax.ppermute(left, "fsdp", [(0, 1), (1, 0)])
        else:
            left = lax.psum(left, "fsdp")
        theirs = after(theirs, own_part, *got_c)
        own_part = own_part + dot(theirs, weight_sibling, ((1,), (0,)))
        own_part, left = lax.optimization_barrier((own_part, left))
        got_e = send(part_e, got_c + [own_part])

        def right_part(got, lo, hi, h0=0, h1=hidden):
            preact = own_part[lo:hi, h0:h1]
            for piece in got:
                preact = preact + piece.astype(F32)
            grad_up = (cot[lo:hi, h0:h1].astype(F32) * jax.nn.silu(preact)).astype(BF16)
            return dot(grad_up, sketch_right[:, h0:h1], ((1,), (1,)))

        rights = [
            right_part(got_a, 0, SEQ, 0, hidden // 2) + right_part(got_b, 0, SEQ, hidden // 2)
        ]
        for got, lo, hi in (
            (got_c, SEQ, 2 * SEQ),
            (got_d, 2 * SEQ, 2 * SEQ + most),
            (got_e, 2 * SEQ + most, 3 * SEQ),
        ):
            rights.append(right_part([after(value, rights[-1], *mark_rows) for value in got], lo, hi))
        marks = jnp.concatenate(mark_rows, axis=0)
        right = jnp.concatenate(rights, axis=0).reshape(examples, SEQ, KB)
        features = jnp.einsum(
            "esa,esb->eab",
            left.reshape(examples, SEQ, KA),
            right,
            precision=lax.Precision.HIGHEST,
        ).reshape(examples, KA * KB)
        high = lax.reduce_precision(features, 8, 7)
        pair = jnp.concatenate([high, features - high], axis=0).astype(BF16)
        panels = dot(pair, marks, ((1,), (1,)))
        scores = panels[:examples] + panels[examples:]

        here = scores.shape[1] // (n_fsdp * n_ckpt)
        scores = scatter_sum(scores.reshape(examples, n_fsdp, n_ckpt * here), "fsdp", n_fsdp)
        return scatter_sum(scores.reshape(examples, n_ckpt, here), "ckpt", n_ckpt)

    return per_device


def solution(mesh):
    in_specs = (
        P("ckpt", "dp", "fsdp"),
        P("ckpt", "dp", "fsdp"),
        P("ckpt", "dp", "fsdp"),
        P(),
        P(None, "fsdp"),
        P("ckpt", "dp", "fsdp"),
    )
    out_specs = P("dp", ("fsdp", "ckpt"))
    per_device = make_per_device(mesh.shape["fsdp"], mesh.shape["ckpt"], mesh.shape["dp"])
    return jax.shard_map(
        per_device, mesh=mesh, in_specs=in_specs, out_specs=out_specs, check_vma=False
    )
```
